32 devices in a mesh: geo: 4 (over y, x), band: 4 (over z), cls: 2 (over core).
Axes of the slice: x: 2, y: 2, z: 4, core: 2. Of those that a mesh axis runs over, the one named last changes fastest.
Arguments:
- mass: bfloat16 [64, 16, 16, 128], P('cls', 'geo', 'band'), may hold values from -6 to 6
- cell_order: int32 [16, 16, 128], P('geo', 'band'), may hold values from 0 to 127, each once within a row
- source_code: int32 [16, 16, 4], P('geo', 'band'), may hold values from 0 to 8
- transport_tiles: bfloat16 [16, 16, 4, 128, 128], P('geo', 'band'), may hold values from -0.25 to 0.25
- ocean_mask: int32 [16, 16], P('geo', 'band'), may hold values 0 or 1
- fragmentation: bfloat16 [64, 64, 16, 16, 128], P(None, None, 'geo', ('band', 'cls')), may hold values from -0.75 to 0.75
Outputs:
- drifted: bfloat16 [64, 16, 16, 128], P('cls', 'geo', 'band')
The draws below stay inside these ranges and needn't reach their ends.
Inputs may be any that keep to these rules, and one draw needn't show every extreme that they name: cell_order holds each of 0..127 once in every tile. `source_code`: codes 0..8 name the 3 x 3 neighbourhood of tiles.
All inputs are finite; a program needn't handle non-finite values. No bound on the sum of `ocean_mask` on one device may be relied on, other than what follows from the above.
Results may differ from the reference program's by a relative error of at most 0.018.
Values may be sent and summed in bfloat16 or wider, within the bound.
A program may use at most 64 MiB of HBM per device.

```python
import jax
import jax.numpy as jnp

CLASSES = 64
TILE = 128
SLOTS = 4
ITERS = 4
NLON = 16
NLAT = 16


def with_ends(array, own_key, least, largest):
    longest = array.shape.index(max(array.shape))
    spots = []
    for shift in (0, 1):
        where = [jax.random.randint(jax.random.fold_in(own_key, axis), (), 0, length) for axis, length in enumerate(array.shape)]
        where[longest] = (where[longest] + shift) % array.shape[longest]
        spots.append(tuple(where))
    return array.at[spots[0]].set(least).at[spots[1]].set(largest)


def block_scale(key, extent, shards, least, top_value):
    loudness = 1.0
    for axis_at, blocks in shards:
        draws = jax.random.uniform(jax.random.fold_in(jax.random.fold_in(key, 6), axis_at), (blocks,), jnp.float32, least / len(shards), top_value / len(shards))
        loudness = loudness * jnp.repeat(jnp.exp(draws), extent[axis_at] // blocks).reshape((-1,) + (1,) * (len(extent) - 1 - axis_at))
    return loudness


def normal_values(own_key, shape, deviation, limit, split=(), held_as=jnp.bfloat16):
    values = jax.random.normal(own_key, shape, jnp.float32) * deviation
    if len(split) > 0:
        values = block_scale(own_key, shape, split, -0.22, 0.18) * values
    return jnp.clip(values, min=-limit, max=limit).astype(held_as)


def setup_inputs(seed: int = 0) -> dict:
    arg_keys = jax.random.split(jax.random.key(seed), 7)
    mass = normal_values(arg_keys[0], (CLASSES, NLON, NLAT, TILE), 1.0, 6.0, ((0, 2), (1, 4), (2, 4)))
    cell_order = jax.vmap(lambda own: jax.random.permutation(own, TILE))(jax.random.split(arg_keys[1], NLON * NLAT)).reshape((NLON, NLAT, TILE)).astype(jnp.int32)
    source_code = with_ends(jax.random.randint(arg_keys[2], (NLON, NLAT, SLOTS), 0, 9), jax.random.fold_in(arg_keys[2], 1), 0, 8).astype(jnp.int32)
    transport_tiles = normal_values(arg_keys[3], (NLON, NLAT, SLOTS, TILE, TILE), (SLOTS * TILE) ** -0.5, 0.25, ((0, 4), (1, 4)))
    ocean_mask = with_ends((jax.random.randint(arg_keys[4], (NLON, NLAT), 0, 4) < 3).astype(jnp.int32), jax.random.fold_in(arg_keys[4], 1), 0, 1)
    fragmentation = normal_values(arg_keys[5], (CLASSES, CLASSES, NLON, NLAT, TILE), CLASSES ** -0.5, 0.75, ((2, 4), (3, 8)))
    return {"mass": mass, "cell_order": cell_order, "source_code": source_code, "transport_tiles": transport_tiles, "ocean_mask": ocean_mask, "fragmentation": fragmentation}


def widen(field):
    wrapped = jnp.concatenate([field[:, -1:], field, field[:, :1]], axis=1)
    return jnp.pad(wrapped, ((0, 0), (0, 0), (1, 1), (0, 0)))


def transport(field, transport_tiles, source_code, ocean_mask):
    padded = widen(field)
    nlon = field.shape[1]
    nlat = field.shape[2]
    total = jnp.zeros(field.shape, jnp.float32)
    for slot in range(transport_tiles.shape[2]):
        picked = jnp.zeros_like(field)
        for code in range(9):
            dlon = code // 3 - 1
            dlat = code % 3 - 1
            view = padded[:, 1 + dlon:1 + dlon + nlon, 1 + dlat:1 + dlat + nlat, :]
            hit = (source_code[:, :, slot] == code)[None, :, :, None]
            picked = jnp.where(hit, view, picked)
        total = total + jnp.einsum("gbij,kgbj->kgbi", transport_tiles[:, :, slot].astype(jnp.float32), picked.astype(jnp.float32))
    keep = ocean_mask.astype(jnp.float32)[None, :, :, None]
    return (total * keep).astype(jnp.bfloat16)


def fragment(fragmentation, moved):
    total = jnp.zeros(moved.shape, jnp.float32)
    for given in range(moved.shape[0]):
        total = total + fragmentation[:, given].astype(jnp.float32) * moved[given].astype(jnp.float32)[None]
    return total.astype(jnp.bfloat16)


def reference(mass, cell_order, source_code, transport_tiles, ocean_mask, fragmentation):
    order = jnp.broadcast_to(cell_order[None], mass.shape).astype(jnp.int32)
    tiled = jnp.take_along_axis(mass, order, axis=3) * ocean_mask.astype(jnp.bfloat16)[None, :, :, None]
    for step in range(ITERS):
        moved = transport(tiled, transport_tiles, source_code, ocean_mask)
        tiled = fragment(fragmentation, moved)
    return tiled
```

```python
import functools

import jax
import jax.numpy as jnp
from jax import lax
from jax.experimental import pallas as pl
from jax.experimental.pallas import tpu as pltpu
from jax.sharding import PartitionSpec as P

ITERS = 4
CHUNKS = 2
DIRECTIONS = [(dx, dy) for dx in (-1, 0, 1) for dy in (-1, 0, 1) if (dx, dy) != (0, 0)]
MESH = pl.DeviceIdType.MESH


def kernel(
    dims, lanes, mass, order, code, tiles, mask, frag, out,
    mass_v, wide, order_v, code_s, mask_s, spot_s, tiles_v, frag_v, moved_f, moved_b, result, fin_send, fin_recv,
    local_sem, pair_send, pair_recv, halo_send, halo_recv, *halo,
):
    per, lon, lat, own_lat, classes, slots, cells = dims
    geo_n, band_n, cls_n = lanes
    own = lon * own_lat
    geo, band, cls = lax.axis_index("geo"), lax.axis_index("band"), lax.axis_index("cls")
    row = band * cls_n + cls
    rows_n = band_n * cls_n
    first_lat = cls * own_lat
    sibling = (geo, band, 1 - cls)

    def place(dx, dy):
        to = row + dy
        return (lax.rem(geo + dx + geo_n, geo_n), to // cls_n, lax.rem(to, cls_n))

    def guarded(dy, body):
        if dy == 0:
            body()
        else:
            pl.when((row + 1 < rows_n) if dy > 0 else (row > 0))(body)

    copies = [
        pltpu.make_async_copy(mass, mass_v.at[cls], local_sem.at[0]),
        pltpu.make_async_copy(order, order_v, local_sem.at[1]),
        pltpu.make_async_copy(code, code_s, local_sem.at[2]),
        pltpu.make_async_copy(mask, mask_s, local_sem.at[3]),
        pltpu.make_async_copy(tiles.at[:, pl.ds(first_lat, own_lat)], tiles_v, local_sem.at[4]),
        pltpu.make_async_copy(frag, frag_v, local_sem.at[5]),
    ]
    for copy in copies:
        copy.start()

    @pl.when(row == 0)
    def _():
        for step in range(ITERS):
            for g in range(lon + 2):
                halo[step][g, 0] = jnp.zeros((classes, cells), jnp.bfloat16)

    @pl.when(row + 1 == rows_n)
    def _():
        for step in range(ITERS):
            for g in range(lon + 2):
                halo[step][g, own_lat + 1] = jnp.zeros((classes, cells), jnp.bfloat16)

    barrier = pltpu.get_barrier_semaphore()
    for dx, dy in DIRECTIONS:
        def greet(dx=dx, dy=dy):
            pl.semaphore_signal(barrier, inc=1, device_id=place(dx, dy), device_id_type=MESH)
        guarded(dy, greet)
    greeted = 2 + 3 * (row > 0).astype(jnp.int32) + 3 * (row + 1 < rows_n).astype(jnp.int32)
    pl.semaphore_wait(barrier, greeted)

    pair = pltpu.make_async_remote_copy(
        src_ref=mass, dst_ref=mass_v.at[cls], send_sem=pair_send.at[0], recv_sem=pair_recv.at[0],
        device_id=sibling, device_id_type=MESH,
    )
    pair.start()
    for copy in copies[:4]:
        copy.wait()
    for g in range(lon):
        for h in range(own_lat):
            for s in range(slots):
                at = (g * own_lat + h) * slots + s
                value = code_s[g, first_lat + h, s]
                third = lax.shift_right_logical(value * 11, 5)
                spot_s[0, at] = g + third
                spot_s[1, at] = h + value - 3 * third
    pair.wait()

    for half in range(cls_n):
        wide[half] = mass_v[half].astype(jnp.float32)
    for g in range(lon):
        for h in range(own_lat):
            line = order_v[g, pl.ds(first_lat + h, 1), :]
            hit = lax.broadcasted_iota(jnp.int32, (cells, cells), 0) == line
            keep = mask_s[g, first_lat + h].astype(jnp.float32)
            picker = jnp.where(hit, keep, 0.0).astype(jnp.bfloat16)
            for half in range(cls_n):
                block = wide[half, pl.ds(g * lat + first_lat + h, per, stride=lon * lat), :]
                placed = jnp.dot(block.astype(jnp.bfloat16), picker, preferred_element_type=jnp.float32)
                halo[0][1 + g, 1 + h, half * per:(half + 1) * per, :] = placed.astype(jnp.bfloat16)

    size = classes // CHUNKS

    def message(step, chunk, way):
        dx, dy = DIRECTIONS[way]
        from_lon = {1: pl.ds(lon, 1), -1: pl.ds(1, 1), 0: pl.ds(1, lon)}[dx]
        to_lon = {1: pl.ds(0, 1), -1: pl.ds(lon + 1, 1), 0: pl.ds(1, lon)}[dx]
        from_lat = {1: pl.ds(own_lat, 1), -1: pl.ds(1, 1), 0: pl.ds(1, own_lat)}[dy]
        to_lat = {1: pl.ds(0, 1), -1: pl.ds(own_lat + 1, 1), 0: pl.ds(1, own_lat)}[dy]
        some = pl.ds(chunk * size, size)
        return pltpu.make_async_remote_copy(
            src_ref=halo[step].at[from_lon, from_lat, some],
            dst_ref=halo[step].at[to_lon, to_lat, some],
            send_sem=halo_send.at[step, chunk, way],
            recv_sem=halo_recv.at[step, chunk, way],
            device_id=place(dx, dy),
            device_id_type=MESH,
        )

    def send(step, chunk):
        for way, (dx, dy) in enumerate(DIRECTIONS):
            guarded(dy, lambda way=way: message(step, chunk, way).start())

    def sent(step, chunk):
        for way, (dx, dy) in enumerate(DIRECTIONS):
            guarded(dy, lambda way=way: message(step, chunk, way).wait_send())

    def arrived(step, chunk):
        for way, (dx, dy) in enumerate(DIRECTIONS):
            guarded(-dy, lambda way=way: message(step, chunk, way).wait_recv())

    def transport(step):
        for chunk in range(CHUNKS):
            arrived(step, chunk)
        for g in range(lon):
            for h in range(own_lat):
                total = None
                for s in range(0, slots, 2):
                    at = (g * own_lat + h) * slots + s
                    left = jnp.concatenate(
                        [halo[step][spot_s[0, at + e], spot_s[1, at + e]] for e in range(2)], axis=1
                    )
                    right = jnp.concatenate([tiles_v[g, h, s + e] for e in range(2)], axis=1)
                    term = lax.dot_general(
                        left, right, (((1,), (1,)), ((), ())), preferred_element_type=jnp.float32
                    )
                    total = term if total is None else total + term
                keep = mask_s[g, first_lat + h].astype(jnp.float32)
                moved_f[pl.ds(g * own_lat + h, classes, stride=own), :] = total * keep
        moved_b[...] = moved_f[...].astype(jnp.bfloat16)

    pack = 16
    blocks = classes * own // pack

    def fragment(start, count):
        together = 4

        def some(at, carry):
            o = start + at * together
            for e in range(together):
                base = pl.multiple_of((o + e) * (classes * own), classes * own)
                total = None
                for q in range(0, blocks, 4):
                    terms = [
                        frag_v[pl.ds(base + (q + j) * pack, pack), :] * moved_b[(q + j) * pack:(q + j + 1) * pack, :]
                        for j in range(4)
                    ]
                    four = ((terms[0] + terms[1]) + (terms[2] + terms[3])).astype(jnp.float32)
                    total = four if total is None else total + four
                result[pl.ds(pl.multiple_of((o + e) * own, own), own), :] = total[:own] + total[own:]
            return carry

        lax.fori_loop(0, count // together, some, 0)

    for chunk in range(CHUNKS):
        send(0, chunk)
    copies[4].wait()
    copies[5].wait()

    def one_step(step):
        transport(step)
        for chunk in range(CHUNKS):
            fragment(chunk * size, size)
            for g in range(lon):
                for h in range(own_lat):
                    values = result[pl.ds(chunk * size * own + g * own_lat + h, size, stride=own), :]
                    halo[step + 1][1 + g, 1 + h, chunk * size:(chunk + 1) * size, :] = values.astype(jnp.bfloat16)
            send(step + 1, chunk)
        for chunk in range(CHUNKS):
            sent(step, chunk)

    for step in range(ITERS - 1):
        one_step(step)

    transport(ITERS - 1)
    fragment((1 - cls) * per, per)
    theirs = pl.ds(pl.multiple_of((1 - cls) * per * own, per * own), per * own)
    fin_send[...] = result[theirs, :].astype(jnp.bfloat16)
    last = pltpu.make_async_remote_copy(
        src_ref=fin_send, dst_ref=fin_recv, send_sem=pair_send.at[1], recv_sem=pair_recv.at[1],
        device_id=sibling, device_id_type=MESH,
    )
    last.start()
    fragment(cls * per, per)
    for chunk in range(CHUNKS):
        sent(ITERS - 1, chunk)
    for h in range(own_lat):
        values = result[pl.ds(cls * per * own + h, per * lon, stride=own_lat), :]
        wide[0, pl.ds(cls * own_lat + h, per * lon, stride=lat), :] = values
    last.wait()
    result[0:per * own, :] = fin_recv[...].astype(jnp.float32)
    for h in range(own_lat):
        values = result[pl.ds(h, per * lon, stride=own_lat), :]
        wide[0, pl.ds((1 - cls) * own_lat + h, per * lon, stride=lat), :] = values
    out[...] = wide[0].astype(out.dtype)


def shards(lanes, mass, cell_order, source_code, transport_tiles, ocean_mask, fragmentation):
    per, lon, lat, cells = mass.shape
    classes = fragmentation.shape[0]
    own_lat = fragmentation.shape[3]
    slots = transport_tiles.shape[2]
    own = lon * own_lat
    dims = (per, lon, lat, own_lat, classes, slots, cells)
    cls_n = lanes[2]
    anywhere = pl.BlockSpec(memory_space=pltpu.HBM)
    result = pl.pallas_call(
        functools.partial(kernel, dims, lanes),
        out_shape=jax.ShapeDtypeStruct((per * lon * lat, cells), jnp.bfloat16),
        in_specs=[anywhere] * 6,
        out_specs=pl.BlockSpec(memory_space=pltpu.VMEM),
        scratch_shapes=[
            pltpu.VMEM((cls_n, per * lon * lat, cells), jnp.bfloat16),
            pltpu.VMEM((cls_n, per * lon * lat, cells), jnp.float32),
            pltpu.VMEM((lon, lat, cells), jnp.int32),
            pltpu.SMEM((lon, lat, slots), jnp.int32),
            pltpu.SMEM((lon, lat), jnp.int32),
            pltpu.SMEM((2, own * slots), jnp.int32),
            pltpu.VMEM((lon, own_lat, slots, cells, cells), jnp.bfloat16),
            pltpu.VMEM((classes * classes * own, cells), jnp.bfloat16),
            pltpu.VMEM((classes * own, cells), jnp.float32),
            pltpu.VMEM((classes * own, cells), jnp.bfloat16),
            pltpu.VMEM((classes * own, cells), jnp.float32),
            pltpu.VMEM((per * own, cells), jnp.bfloat16),
            pltpu.VMEM((per * own, cells), jnp.bfloat16),
            pltpu.SemaphoreType.DMA((6,)),
            pltpu.SemaphoreType.DMA((2,)),
            pltpu.SemaphoreType.DMA((2,)),
            pltpu.SemaphoreType.DMA((ITERS, CHUNKS, len(DIRECTIONS))),
            pltpu.SemaphoreType.DMA((ITERS, CHUNKS, len(DIRECTIONS))),
        ] + [pltpu.VMEM((lon + 2, own_lat + 2, classes, cells), jnp.bfloat16)] * ITERS,
        compiler_params=pltpu.CompilerParams(
            collective_id=0, has_side_effects=True, vmem_limit_bytes=56 * 1024 * 1024
        ),
    )(
        mass.reshape(per * lon * lat, cells),
        cell_order,
        source_code,
        transport_tiles,
        ocean_mask,
        fragmentation.reshape(classes * classes * own, cells),
    )
    return result.reshape(per, lon, lat, cells)


def solution(mesh):
    placed = (
        P("cls", "geo", "band", None),
        P("geo", "band", None),
        P("geo", "band", None),
        P("geo", "band", None, None, None),
        P("geo", "band"),
        P(None, None, "geo", ("band", "cls"), None),
    )
    lanes = (mesh.shape["geo"], mesh.shape["band"], mesh.shape["cls"])
    return jax.shard_map(
        functools.partial(shards, lanes),
        mesh=mesh, in_specs=placed, out_specs=P("cls", "geo", "band", None), check_vma=False,
    )
```

```python
import functools

import jax
import jax.numpy as jnp
from jax import lax
from jax.experimental import pallas as pl
from jax.experimental.pallas import tpu as pltpu
from jax.sharding import PartitionSpec as P

ITERS = 4
CHUNKS = 2
DIRECTIONS = [(dx, dy) for dx in (-1, 0, 1) for dy in (-1, 0, 1) if (dx, dy) != (0, 0)]
MESH = pl.DeviceIdType.MESH


def kernel(
    dims, lanes, mass, order, code, tiles, mask, frag, out,
    mass_v, wide, order_v, code_s, mask_s, spot_s, tiles_v, frag_v, moved_f, result, fin_send, fin_recv,
    local_sem, pair_send, pair_recv, halo_send, halo_recv, *halo,
):
    per, lon, lat, own_lat, classes, slots, cells = dims
    geo_n, band_n, cls_n = lanes
    own = lon * own_lat
    size = classes // CHUNKS
    geo, band, cls = lax.axis_index("geo"), lax.axis_index("band"), lax.axis_index("cls")
    row = band * cls_n + cls
    rows_n = band_n * cls_n
    first_lat = cls * own_lat
    sibling = (geo, band, 1 - cls)

    def place(dx, dy):
        to = row + dy
        return (lax.rem(geo + dx + geo_n, geo_n), to // cls_n, lax.rem(to, cls_n))

    def guarded(dy, body):
        if dy == 0:
            body()
        else:
            pl.when((row + 1 < rows_n) if dy > 0 else (row > 0))(body)

    copies = [
        pltpu.make_async_copy(mass, mass_v.at[cls], local_sem.at[0]),
        pltpu.make_async_copy(order, order_v, local_sem.at[1]),
        pltpu.make_async_copy(code, code_s, local_sem.at[2]),
        pltpu.make_async_copy(mask, mask_s, local_sem.at[3]),
        pltpu.make_async_copy(tiles.at[:, pl.ds(first_lat, own_lat)], tiles_v, local_sem.at[4]),
        pltpu.make_async_copy(frag, frag_v, local_sem.at[5]),
    ]
    for copy in copies:
        copy.start()

    @pl.when(row == 0)
    def _():
        for buffer in halo:
            for g in range(lon + 2):
                buffer[g, 0] = jnp.zeros((size, cells), jnp.bfloat16)

    @pl.when(row + 1 == rows_n)
    def _():
        for buffer in halo:
            for g in range(lon + 2):
                buffer[g, own_lat + 1] = jnp.zeros((size, cells), jnp.bfloat16)

    barrier = pltpu.get_barrier_semaphore()
    for dx, dy in DIRECTIONS:
        def greet(dx=dx, dy=dy):
            pl.semaphore_signal(barrier, inc=1, device_id=place(dx, dy), device_id_type=MESH)
        guarded(dy, greet)
    copies[4].wait()
    for g in range(lon):
        for h in range(own_lat):
            for s in range(slots):
                tiles_v[g, h, s] = tiles_v[g, h, s].T
    greeted = 2 + 3 * (row > 0).astype(jnp.int32) + 3 * (row + 1 < rows_n).astype(jnp.int32)
    pl.semaphore_wait(barrier, greeted)

    pair = pltpu.make_async_remote_copy(
        src_ref=mass, dst_ref=mass_v.at[cls], send_sem=pair_send.at[0], recv_sem=pair_recv.at[0],
        device_id=sibling, device_id_type=MESH,
    )
    pair.start()
    for copy in copies[:4]:
        copy.wait()
    for g in range(lon):
        for h in range(own_lat):
            for s in range(slots):
                at = (g * own_lat + h) * slots + s
                value = code_s[g, first_lat + h, s]
                third = lax.shift_right_logical(value * 11, 5)
                spot_s[0, at] = g + third
                spot_s[1, at] = h + value - 3 * third
    pair.wait()

    for half in range(cls_n):
        wide[half] = mass_v[half].astype(jnp.float32)
    for g in range(lon):
        for h in range(own_lat):
            line = order_v[g, pl.ds(first_lat + h, 1), :]
            hit = lax.broadcasted_iota(jnp.int32, (cells, cells), 0) == line
            keep = mask_s[g, first_lat + h].astype(jnp.float32)
            picker = jnp.where(hit, keep, 0.0).astype(jnp.bfloat16)
            for half in range(cls_n):
                block = wide[half, pl.ds(g * lat + first_lat + h, per, stride=lon * lat), :]
                placed = jnp.dot(block.astype(jnp.bfloat16), picker, preferred_element_type=jnp.float32)
                halo[half * per // size][1 + g, 1 + h, half * per % size:half * per % size + per, :] = placed.astype(jnp.bfloat16)

    def message(step, chunk, way):
        dx, dy = DIRECTIONS[way]
        from_lon = {1: pl.ds(lon, 1), -1: pl.ds(1, 1), 0: pl.ds(1, lon)}[dx]
        to_lon = {1: pl.ds(0, 1), -1: pl.ds(lon + 1, 1), 0: pl.ds(1, lon)}[dx]
        from_lat = {1: pl.ds(own_lat, 1), -1: pl.ds(1, 1), 0: pl.ds(1, own_lat)}[dy]
        to_lat = {1: pl.ds(0, 1), -1: pl.ds(own_lat + 1, 1), 0: pl.ds(1, own_lat)}[dy]
        buffer = halo[step * CHUNKS + chunk]
        return pltpu.make_async_remote_copy(
            src_ref=buffer.at[from_lon, from_lat],
            dst_ref=buffer.at[to_lon, to_lat],
            send_sem=halo_send.at[step, chunk, way],
            recv_sem=halo_recv.at[step, chunk, way],
            device_id=place(dx, dy),
            device_id_type=MESH,
        )

    def send(step, chunk):
        for way, (dx, dy) in enumerate(DIRECTIONS):
            guarded(dy, lambda way=way: message(step, chunk, way).start())

    def sent(step, chunk):
        for way, (dx, dy) in enumerate(DIRECTIONS):
            guarded(dy, lambda way=way: message(step, chunk, way).wait_send())

    def arrived(step, chunk):
        for way, (dx, dy) in enumerate(DIRECTIONS):
            guarded(-dy, lambda way=way: message(step, chunk, way).wait_recv())

    def transport(step, chunk):
        arrived(step, chunk)
        buffer = halo[step * CHUNKS + chunk]
        for g in range(lon):
            for h in range(own_lat):
                total = None
                for s in range(0, slots, 2):
                    at = (g * own_lat + h) * slots + s
                    left = jnp.concatenate(
                        [buffer[spot_s[0, at + e], spot_s[1, at + e]] for e in range(2)], axis=1
                    )
                    right = jnp.concatenate([tiles_v[g, h, s + e] for e in range(2)], axis=0)
                    term = lax.dot_general(
                        left, right, (((1,), (0,)), ((), ())), preferred_element_type=jnp.float32
                    )
                    total = term if total is None else total + term
                keep = mask_s[g, first_lat + h].astype(jnp.float32)
                moved_f[pl.ds(g * own_lat + h, size, stride=own), :] = total * keep

    pack = 16
    blocks = size * own // pack

    def fragment(chunk, start, count):
        together = 8
        moved = moved_f[...].astype(jnp.bfloat16)

        def some(at, carry):
            for e in range(together):
                o = start + at * together + e
                base = pl.multiple_of((o * classes + chunk * size) * own, size * own)
                total = None
                block = frag_v[pl.ds(base, size * own), :] * moved
                half = block[:size * own // 2] + block[size * own // 2:]
                half = (half[:size * own // 4] + half[size * own // 4:]).astype(jnp.float32)
                for q in range(0, blocks // 4):
                    four = half[q * pack:(q + 1) * pack]
                    total = four if total is None else total + four
                spot = pl.ds(pl.multiple_of(o * own, own), own)
                total = total[:own] + total[own:]
                result[spot, :] = total if chunk == 0 else result[spot, :] + total
            return carry

        lax.fori_loop(0, count // together, some, 0)

    for chunk in range(CHUNKS):
        send(0, chunk)
    copies[5].wait()

    def early(step):
        for chunk in range(CHUNKS - 1):
            transport(step, chunk)
            fragment(chunk, 0, classes)
        transport(step, CHUNKS - 1)

    for step in range(ITERS - 1):
        early(step)
        for chunk in range(CHUNKS):
            fragment(CHUNKS - 1, chunk * size, size)
            for g in range(lon):
                for h in range(own_lat):
                    values = result[pl.ds(chunk * size * own + g * own_lat + h, size, stride=own), :]
                    halo[(step + 1) * CHUNKS + chunk][1 + g, 1 + h] = values.astype(jnp.bfloat16)
            send(step + 1, chunk)
        for chunk in range(CHUNKS):
            sent(step, chunk)

    early(ITERS - 1)

    def half_of(which):
        return result[pl.ds(pl.multiple_of(which * per * own, per * own), per * own), :].astype(jnp.bfloat16)

    fragment(CHUNKS - 1, (1 - cls) * per, per)
    fin_send[...] = half_of(1 - cls)
    last = pltpu.make_async_remote_copy(
        src_ref=fin_send, dst_ref=fin_recv, send_sem=pair_send.at[1], recv_sem=pair_recv.at[1],
        device_id=sibling, device_id_type=MESH,
    )
    last.start()
    fragment(CHUNKS - 1, cls * per, per)
    out[cls] = half_of(cls)
    for chunk in range(CHUNKS):
        sent(ITERS - 1, chunk)
    last.wait()
    out[1 - cls] = fin_recv[...]


def shards(lanes, mass, cell_order, source_code, transport_tiles, ocean_mask, fragmentation):
    per, lon, lat, cells = mass.shape
    classes = fragmentation.shape[0]
    own_lat = fragmentation.shape[3]
    slots = transport_tiles.shape[2]
    own = lon * own_lat
    dims = (per, lon, lat, own_lat, classes, slots, cells)
    cls_n = lanes[2]
    anywhere = pl.BlockSpec(memory_space=pltpu.HBM)
    result = pl.pallas_call(
        functools.partial(kernel, dims, lanes),
        out_shape=jax.ShapeDtypeStruct((cls_n, per * own, cells), jnp.bfloat16),
        in_specs=[anywhere] * 6,
        out_specs=pl.BlockSpec(memory_space=pltpu.VMEM),
        scratch_shapes=[
            pltpu.VMEM((cls_n, per * lon * lat, cells), jnp.bfloat16),
            pltpu.VMEM((cls_n, per * lon * lat, cells), jnp.float32),
            pltpu.VMEM((lon, lat, cells), jnp.int32),
            pltpu.SMEM((lon, lat, slots), jnp.int32),
            pltpu.SMEM((lon, lat), jnp.int32),
            pltpu.SMEM((2, own * slots), jnp.int32),
            pltpu.VMEM((lon, own_lat, slots, cells, cells), jnp.bfloat16),
            pltpu.VMEM((classes * classes * own, cells), jnp.bfloat16),
            pltpu.VMEM((classes // CHUNKS * own, cells), jnp.float32),
            pltpu.VMEM((classes * own, cells), jnp.float32),
            pltpu.VMEM((per * own, cells), jnp.bfloat16),
            pltpu.VMEM((per * own, cells), jnp.bfloat16),
            pltpu.SemaphoreType.DMA((6,)),
            pltpu.SemaphoreType.DMA((2,)),
            pltpu.SemaphoreType.DMA((2,)),
            pltpu.SemaphoreType.DMA((ITERS, CHUNKS, len(DIRECTIONS))),
            pltpu.SemaphoreType.DMA((ITERS, CHUNKS, len(DIRECTIONS))),
        ] + [pltpu.VMEM((lon + 2, own_lat + 2, classes // CHUNKS, cells), jnp.bfloat16)] * (ITERS * CHUNKS),
        compiler_params=pltpu.CompilerParams(
            collective_id=0, has_side_effects=True, vmem_limit_bytes=56 * 1024 * 1024
        ),
    )(
        mass.reshape(per * lon * lat, cells),
        cell_order,
        source_code,
        transport_tiles,
        ocean_mask,
        fragmentation.reshape(classes * classes * own, cells),
    )
    result = result.reshape(cls_n, per, lon, own_lat, cells)
    return jnp.moveaxis(result, 0, 2).reshape(per, lon, lat, cells)


def solution(mesh):
    placed = (
        P("cls", "geo", "band", None),
        P("geo", "band", None),
        P("geo", "band", None),
        P("geo", "band", None, None, None),
        P("geo", "band"),
        P(None, None, "geo", ("band", "cls"), None),
    )
    lanes = (mesh.shape["geo"], mesh.shape["band"], mesh.shape["cls"])
    return jax.shard_map(
        functools.partial(shards, lanes),
        mesh=mesh, in_specs=placed, out_specs=P("cls", "geo", "band", None), check_vma=False,
    )
```
